32 devices in a mesh: space: 16 (over z, y, x), vec: 2 (over core).
Axes of the slice: x: 2, y: 2, z: 4, core: 2. Of those that a mesh axis runs over, the one named last changes fastest.
Arguments:
- potential: float32 [16, 128, 256], P('space'), may hold values from -8.25 to 8.25
- start_basis: float32 [16, 16, 128, 256], P('vec', 'space'), may hold values from -6 to 6
Outputs:
- new_basis: float32 [16, 16, 128, 256], P('vec', 'space')
- rayleigh: float32 [16, 16], replicated
The draws below stay inside these ranges and needn't reach their ends.
All inputs are finite; a program needn't handle non-finite values.
Results may differ from the reference program's by a relative error of at most 0.0003.
Values sent between devices are 32-bit elements; how exact they have to be, the bound alone decides.
A program may use at most 64 MiB of HBM per device.

```python
import jax
import jax.numpy as jnp
from jax import lax

NB = 16
LY = 128
LX = 256
NSWEEP = 3
NZ = 16


def block_scale(stream_key, extent, cuts, smallest, top_value):
    def one(dim, parts):
        draws = jax.random.uniform(jax.random.fold_in(jax.random.fold_in(stream_key, 6), dim), (parts,), jnp.float32, smallest / len(cuts), top_value / len(cuts))
        return jnp.repeat(jnp.exp(draws), extent[dim] // parts).reshape((-1,) + (1,) * (len(extent) - dim - 1))

    gain = one(*cuts[0])
    for cut in cuts[1:]:
        gain = gain * one(*cut)
    return gain


def scatter_about(rng, extent, scale, reach, pieces=(), held_as=jnp.bfloat16):
    factor_of = block_scale(rng, extent, pieces, -0.22, 0.18) if pieces else 1.0
    array = jax.random.normal(rng, extent, jnp.float32) * scale * factor_of
    return jnp.minimum(jnp.maximum(array, -reach), reach).astype(held_as)


def setup_inputs(seed: int = 0) -> dict:
    arg_keys = jax.random.split(jax.random.key(seed), 3)
    potential = jnp.clip(jax.random.uniform(arg_keys[0], (NZ, LY, LX), jnp.float32, -8.25, 8.25) * block_scale(arg_keys[0], (NZ, LY, LX), ((0, 16),), -0.4, 0.0), -8.25, 8.25)
    start_basis = scatter_about(arg_keys[1], (NB, NZ, LY, LX), 1.0, 6.0, ((0, 2), (1, 16)), jnp.float32)
    return {"potential": potential, "start_basis": start_basis}


SIGMA = 0.5
PREC = lax.Precision.HIGHEST

def inner(left, right):
    total = jnp.einsum('kzyx,jzyx->kj', left, right, precision=PREC)
    return total / (left.shape[1] * left.shape[2] * left.shape[3])

def combine(coeff, vectors):
    return jnp.einsum('kj,kzyx->jzyx', coeff, vectors, precision=PREC)

def hamilton(field, potential):
    beside = jnp.roll(field, 1, 1) + jnp.roll(field, -1, 1)
    beside = beside + jnp.roll(field, 1, 2) + jnp.roll(field, -1, 2)
    beside = beside + jnp.roll(field, 1, 3) + jnp.roll(field, -1, 3)
    return potential * field - beside

def orthonormal(block, gram):
    lower = jnp.linalg.cholesky(gram)
    inverse = jax.scipy.linalg.solve_triangular(lower, jnp.eye(gram.shape[0], dtype=jnp.float32), lower=True)
    return combine(inverse.T, block)

def reference(potential, start_basis):
    basis = orthonormal(start_basis, inner(start_basis, start_basis))
    image = hamilton(basis, potential)
    rayleigh = inner(basis, image)
    resid = image - combine(rayleigh, basis)
    shifted = jnp.where(potential >= SIGMA, potential - SIGMA + 6.0, potential - SIGMA - 6.0)
    correction = jnp.zeros_like(basis)
    for sweep in range(NSWEEP):
        coeff = inner(basis, correction)
        proj = correction - combine(coeff, basis)
        moved = hamilton(proj, potential) - SIGMA * proj
        back = inner(basis, moved)
        correction = correction + (-resid - (moved - combine(back, basis))) / shifted
    proj_two = inner(basis, correction)
    fresh = correction - combine(proj_two, basis)
    new_basis = orthonormal(fresh, inner(fresh, fresh))
    return (new_basis, rayleigh)
```

```python
import functools

import jax
import jax.numpy as jnp
from jax import lax
from jax.experimental import pallas as pl
from jax.experimental.pallas import tpu as pltpu
from jax.sharding import PartitionSpec as P

NSWEEP = 3


SIGMA = 0.5
PREC = lax.Precision.HIGHEST


def extended(value, sides, width):
    for axis, dim in sides:
        peers, length = (lax.axis_size(axis), value.shape[dim])
        up = [(i, (i + 1) % peers) for i in range(peers)]
        down = [(j, i) for i, j in up]
        last = lax.slice_in_dim(value, length - width, length, axis=dim)
        first = lax.slice_in_dim(value, 0, width, axis=dim)
        before = lax.ppermute(last, axis, up)
        after = lax.ppermute(first, axis, down)
        value = jnp.concatenate([before, value, after], axis=dim)
    return value


def local_inner(left, right, scale):
    return jnp.einsum("kzyx,jzyx->kj", left, right, precision=PREC) * scale


def combine(coeff, vectors):
    return jnp.einsum("kj,kzyx->jzyx", coeff, vectors, precision=PREC)


def stencil(padded, potential):
    center = padded[:, 1:-1]
    beside = padded[:, 2:] + padded[:, :-2]
    beside = beside + jnp.roll(center, 1, 2) + jnp.roll(center, -1, 2)
    beside = beside + jnp.roll(center, 1, 3) + jnp.roll(center, -1, 3)
    return potential * center - beside


def inverse_factor(gram):
    lower = jnp.linalg.cholesky(gram)
    return jax.scipy.linalg.solve_triangular(
        lower, jnp.eye(gram.shape[0], dtype=jnp.float32), lower=True
    )


def local(potential, start_basis):
    mine = start_basis.shape[0]
    scale = 1.0 / (
        start_basis.shape[1] * start_basis.shape[2] * start_basis.shape[3] * lax.axis_size("space")
    )
    first = lax.axis_index("vec") * mine
    whole = lax.all_gather(start_basis, "vec", axis=0, tiled=True)
    gram = lax.psum(local_inner(whole, whole, scale), "space")
    basis_all = combine(inverse_factor(gram).T, whole)
    basis = lax.dynamic_slice_in_dim(basis_all, first, mine, 0)
    shifted = jnp.where(potential >= SIGMA, potential - SIGMA + 6.0, potential - SIGMA - 6.0)
    padded = extended(basis_all, (("space", 1),), 1)
    image_all = stencil(padded, potential)
    rayleigh = lax.psum(local_inner(basis_all, image_all, scale), "space")
    image = lax.dynamic_slice_in_dim(image_all, first, mine, 0)
    panel_mine = lax.dynamic_slice_in_dim(rayleigh, first, mine, 1)
    resid = image - combine(panel_mine, basis_all)
    correction = jnp.zeros_like(basis)
    for sweep in range(NSWEEP):
        coeff, cross = lax.psum(
            (local_inner(basis_all, correction, scale), local_inner(image_all, correction, scale)),
            "space",
        )
        padded = extended(correction, (("space", 1),), 1)
        proj = correction - combine(coeff, basis_all)
        moved = stencil(padded, potential) - combine(coeff, image_all) - SIGMA * proj
        back = cross - jnp.dot(rayleigh.T, coeff, precision=PREC)
        update = -resid - (moved - combine(back, basis_all))
        correction = correction + update / shifted
    proj_two = lax.psum(local_inner(basis_all, correction, scale), "space")
    fresh = correction - combine(proj_two, basis_all)
    fresh_all = lax.all_gather(fresh, "vec", axis=0, tiled=True)
    gram_two = lax.psum(local_inner(fresh_all, fresh_all, scale), "space")
    inverse_two = inverse_factor(gram_two)
    rows_mine = lax.dynamic_slice_in_dim(inverse_two, first, mine, 0)
    new_basis = combine(rows_mine.T, fresh_all)
    return (new_basis, rayleigh)


MESH = pl.DeviceIdType.MESH
F32 = jnp.float32
BF16 = jnp.bfloat16
NN = (((1,), (0,)), ((), ()))
NT = (((1,), (1,)), ((), ()))
TN = (((0,), (0,)), ((), ()))


def small(a, b, dims=NN):
    return lax.dot_general(a, b, dims, precision=PREC, preferred_element_type=F32)


def split(a):
    high = a.astype(BF16)
    return high, (a - high.astype(F32)).astype(BF16)


def dot3(a, b, dims=NN):
    (ah, al), (bh, bl) = a, b

    def one(p, q):
        return lax.dot_general(p, q, dims, preferred_element_type=F32)

    return one(ah, bh) + (one(ah, bl) + one(al, bh))


def tile_of(space):
    z, y, x = space // 4, (space // 2) % 2, space % 2
    q = 2 * y + (x + y) % 2
    return 4 * q + z + (q % 2) * (3 - 2 * z)


def space_of(tile):
    q, r = tile // 4, tile % 4
    z = r + (q % 2) * (3 - 2 * r)
    return z * 4 + (q // 2) * 2 + ((q + 1) // 2) % 2


def factor_inverse(gram):
    n = gram.shape[0]
    rows = lax.broadcasted_iota(jnp.int32, (n, n), 0)
    cols = lax.broadcasted_iota(jnp.int32, (n, n), 1)
    eye = jnp.where(rows == cols, 1.0, 0.0).astype(F32)
    upper, inv = gram, eye
    row = lax.broadcasted_iota(jnp.int32, (n, 1), 0)
    for k in range(n - 1):
        mult = jnp.where(row > k, upper[:, k : k + 1] / upper[k : k + 1, k : k + 1], 0.0)
        inv = inv - mult * inv[k : k + 1, :]
        upper = upper - mult * upper[k : k + 1, :]
    diag = jnp.sum(upper * eye, axis=1, keepdims=True)
    return inv / jnp.sqrt(diag)


def kernel(
    nb, scale,
    pot_in, s_in, out_ref, ray_ref,
    pot, dinv, fs, f1, f2, ft, fq, ysend, yrecv, acc, red1, red2,
    in_send, in_recv, pot_send, pot_recv, halo_send, halo_recv,
    r1_send, r1_recv, r2_send, r2_recv, out_send, out_recv,
):
    s, v = lax.axis_index("space"), lax.axis_index("vec")
    tile = tile_of(s)
    half = s // 8
    me = s * 2 + v
    rows8 = nb * 8

    barrier = pltpu.get_barrier_semaphore()

    def greet(i, _):
        peer = (me + i) % 32
        pl.semaphore_signal(barrier, inc=1, device_id=(peer // 2, peer % 2), device_id_type=MESH)
        return 0

    lax.fori_loop(1, 32, greet, 0)
    pl.semaphore_wait(barrier, 31)

    def s_piece(dest):
        return s_in.at[:, 0, pl.ds(pl.multiple_of(tile_of(dest) * 8, 8), 8), :]

    s_slot = fs.at[1 + s % 8, pl.ds(v * 8, 8)]

    def pot_piece(dest):
        return pot_in.at[0, pl.ds(pl.multiple_of(tile_of(dest) * 8, 8), 8), :]

    def s_copy(o):
        dest = (s + o) % 16
        return pltpu.make_async_remote_copy(
            src_ref=s_piece(dest), dst_ref=s_slot,
            send_sem=in_send.at[o], recv_sem=in_recv.at[s % 8, v],
            device_id=(dest, half), device_id_type=MESH,
        )

    def pot_copy(o):
        dest = (s + o) % 16
        return pltpu.make_async_remote_copy(
            src_ref=pot_piece(dest), dst_ref=pot.at[s % 8],
            send_sem=pot_send.at[o], recv_sem=pot_recv.at[s % 8],
            device_id=(dest, half), device_id_type=MESH,
        )

    def send_in(o, _):
        s_copy(o).start()

        @pl.when(half == v)
        def _():
            pot_copy(o).start()

        return 0

    lax.fori_loop(1, 16, send_in, 0)

    @pl.when(half == v)
    def _():
        pltpu.make_async_copy(s_piece(s), s_slot, in_recv.at[s % 8, v]).start()
        pltpu.make_async_copy(pot_piece(s), pot.at[s % 8], pot_recv.at[s % 8]).start()

    @pl.when(half != v)
    def _():
        s_copy(0).start()

    def done_in(z, _):
        for w in range(2):
            slot = fs.at[1 + z, pl.ds(w * 8, 8)]
            pltpu.make_async_copy(slot, slot, in_recv.at[z, w]).wait()
        pltpu.make_async_copy(pot.at[z], pot.at[z], pot_recv.at[z]).wait()
        return 0

    lax.fori_loop(0, 8, done_in, 0)

    after = space_of((tile + 1) % 16)
    before = space_of((tile + 15) % 16)

    def halo(n, field):
        def pack(z, _):
            ysend[n, 0, z] = field[1 + z, :, 7:8, :]
            ysend[n, 1, z] = field[1 + z, :, 0:1, :]
            return 0

        def copy(i, src, dst, device):
            return pltpu.make_async_remote_copy(
                src_ref=src, dst_ref=dst,
                send_sem=halo_send.at[n, i], recv_sem=halo_recv.at[n, i],
                device_id=device, device_id_type=MESH,
            )

        lax.fori_loop(0, 8, pack, 0)
        copies = [
            copy(0, ysend.at[n, 0], yrecv.at[n, 0], (after, v)),
            copy(1, ysend.at[n, 1], yrecv.at[n, 1], (before, v)),
            copy(2, field.at[1], field.at[9], (s, 1 - v)),
            copy(3, field.at[8], field.at[0], (s, 1 - v)),
        ]
        for c in copies:
            c.start()
        for c in copies:
            c.wait()

    inrow = lax.broadcasted_iota(jnp.int32, (rows8, 256), 0) % 8
    is_first, is_last = inrow == 0, inrow == 7

    def flat(a):
        return jnp.broadcast_to(a, (nb, 8, 256)).reshape(rows8, 256)

    def get(field, z):
        return field[z].reshape(rows8, 256)

    def put(field, z, value):
        field[z] = value.reshape(nb, 8, 256)

    def apply_h(n, field, z):
        mid = get(field, z + 1)
        total = get(field, z) + get(field, z + 2)
        total += jnp.where(is_first, flat(yrecv[n, 0, z]), pltpu.roll(mid, 1, 0))
        total += jnp.where(is_last, flat(yrecv[n, 1, z]), pltpu.roll(mid, rows8 - 1, 0))
        total += pltpu.roll(mid, 1, 1) + pltpu.roll(mid, 255, 1)
        return mid, flat(pot[z][None]) * mid - total

    er = lax.broadcasted_iota(jnp.int32, (rows8, nb), 0) // 8
    ec = lax.broadcasted_iota(jnp.int32, (rows8, nb), 1)
    expand = jnp.where(er == ec, 1.0, 0.0).astype(F32)
    kr = lax.broadcasted_iota(jnp.int32, (rows8, rows8), 0) % 8
    kc = lax.broadcasted_iota(jnp.int32, (rows8, rows8), 1) % 8
    same_row = kr == kc

    def kron(matrix, dims=NT):
        wide = small(small(expand, matrix, dims), expand, NT)
        return split(jnp.where(same_row, wide, 0.0))

    def squeeze(i):
        kept = jnp.where(same_row, acc[i], 0.0)
        return small(small(expand, kept, TN), expand) * scale

    def total_of(n, parts):
        rank = (s % 4) * 2 + v
        for i, part in enumerate(parts):
            red1[n, rank, i] = part

        used = len(parts)

        def copy1(i):
            peer = (rank + i) % 8
            return pltpu.make_async_remote_copy(
                src_ref=red1.at[n, rank, pl.ds(0, used)], dst_ref=red1.at[n, rank, pl.ds(0, used)],
                send_sem=r1_send.at[n, i], recv_sem=r1_recv.at[n, rank],
                device_id=((s // 4) * 4 + peer // 2, peer % 2), device_id_type=MESH,
            )

        def copy2(i):
            peer = (s // 4 + i) % 4
            return pltpu.make_async_remote_copy(
                src_ref=red2.at[n, s // 4, pl.ds(0, used)], dst_ref=red2.at[n, s // 4, pl.ds(0, used)],
                send_sem=r2_send.at[n, i], recv_sem=r2_recv.at[n, s // 4],
                device_id=(peer * 4 + s % 4, v), device_id_type=MESH,
            )

        def stage(copy, buf, recv, mine, count):
            for i in range(1, count):
                copy(i).start()
            for i in range(1, count):
                peer = (mine + i) % count
                slot = buf.at[n, peer, pl.ds(0, used)]
                pltpu.make_async_copy(slot, slot, recv.at[n, peer]).wait()
            for i in range(1, count):
                copy(i).wait_send()
            sums = []
            for i in range(used):
                total = buf[n, 0, i]
                for p in range(1, count):
                    total = total + buf[n, p, i]
                sums.append(total)
            return sums

        sums = stage(copy1, red1, r1_recv, rank, 8)
        for i, part in enumerate(sums):
            red2[n, s // 4, i] = part
        return stage(copy2, red2, r2_recv, s // 4, 4)

    def clear(count):
        for i in range(count):
            acc[i] = jnp.zeros((rows8, rows8), F32)

    halo(0, fs)
    clear(5)

    def first(z, _):
        mid, image = apply_h(0, fs, z)
        put(ft, z, image)
        p = pot[z]
        inverse = 1.0 / jnp.where(p >= SIGMA, p - SIGMA + 6.0, p - SIGMA - 6.0)
        dinv[z] = inverse
        wide = flat(inverse[None])
        a, b = split(mid), split(image)
        c, d = split(wide * mid), split(wide * image)
        acc[0] += dot3(a, a, NT)
        acc[1] += dot3(a, b, NT)
        acc[2] += dot3(a, c, NT)
        acc[3] += dot3(a, d, NT)
        acc[4] += dot3(b, d, NT)
        return 0

    lax.fori_loop(0, 8, first, 0)
    gram, raw, m0, m1, m2 = total_of(0, [squeeze(i) for i in range(5)])
    w = factor_inverse(gram)

    def conj(m):
        return small(small(w, m), w, NT)

    ray, n0, n1, n2 = conj(raw), conj(m0), conj(m1), conj(m2)
    ray_ref[...] = ray
    coeff = small(n0, ray) - n1
    cross = small(n1, ray, TN) - n2
    edge = cross - small(ray, coeff, TN) - SIGMA * coeff

    kw, kray = kron(w, NN), kron(ray)

    def second(z, _):
        basis = dot3(kw, split(get(fs, z + 1)))
        image = dot3(kw, split(get(ft, z)))
        put(fs, z + 1, basis)
        put(ft, z, image)
        put(f1, z + 1, flat(dinv[z][None]) * (dot3(kray, split(basis)) - image))
        return 0

    lax.fori_loop(0, 8, second, 0)
    halo(1, f1)
    kco, ked = kron(coeff), kron(edge)

    def third(z, _):
        mid, image = apply_h(1, f1, z)
        mix = dot3(kco, split(get(ft, z))) + dot3(ked, split(get(fs, z + 1)))
        put(f2, z + 1, 2.0 * mid + flat(dinv[z][None]) * (SIGMA * mid - image + mix))
        return 0

    lax.fori_loop(0, 8, third, 0)
    halo(2, f2)
    clear(3)

    def fourth(z, _):
        mid, image = apply_h(2, f2, z)
        new = mid + get(f1, z + 1) + flat(dinv[z][None]) * (SIGMA * mid - image)
        put(fq, z, new)
        a, b = split(get(fs, z + 1)), split(get(ft, z))
        c, d = split(mid), split(new)
        acc[0] += dot3(a, c, NT)
        acc[1] += dot3(b, c, NT)
        acc[2] += dot3(a, d, NT)
        return 0

    lax.fori_loop(0, 8, fourth, 0)
    coeff, cross, part = total_of(1, [squeeze(i) for i in range(3)])
    edge = cross - small(ray, coeff, TN) - SIGMA * coeff
    proj = part + small(n1, coeff) + small(n0, edge)
    kco, ked, kpr = kron(coeff), kron(edge), kron(proj)
    clear(1)

    def fifth(z, _):
        basis = split(get(fs, z + 1))
        mix = dot3(kco, split(get(ft, z))) + dot3(ked, basis)
        fresh = get(fq, z) + flat(dinv[z][None]) * mix - dot3(kpr, basis)
        put(fq, z, fresh)
        a = split(fresh)
        acc[0] += dot3(a, a, NT)
        return 0

    lax.fori_loop(0, 8, fifth, 0)
    (gram2,) = total_of(2, [squeeze(0)])
    kw2 = kron(factor_inverse(gram2), NN)

    out_rows = out_ref.at[:, 0, pl.ds(pl.multiple_of(tile * 8, 8), 8), :]

    def out_copy(z, w):
        return pltpu.make_async_remote_copy(
            src_ref=fq.at[z, pl.ds(w * 8, 8)], dst_ref=out_rows,
            send_sem=out_send.at[z, w], recv_sem=out_recv.at[tile],
            device_id=(v * 8 + z, w), device_id_type=MESH,
        )

    def last(i, _):
        z = (tile + i) % 8
        put(fq, z, dot3(kw2, split(get(fq, z))))
        for w in range(2):
            mine = (v * 8 + z) * 2 + w == me

            @pl.when(mine)
            def _():
                pltpu.make_async_copy(
                    fq.at[z, pl.ds(w * 8, 8)], out_rows, out_recv.at[tile]
                ).start()

            @pl.when(jnp.logical_not(mine))
            def _():
                out_copy(z, w).start()

        return 0

    lax.fori_loop(0, 8, last, 0)

    def drain_in(o, _):
        s_copy(o).wait_send()

        @pl.when(half == v)
        def _():
            pot_copy(o).wait_send()

        return 0

    lax.fori_loop(1, 16, drain_in, 0)

    @pl.when(half != v)
    def _():
        s_copy(0).wait_send()

    def drain_out(z, _):
        for w in range(2):
            @pl.when((v * 8 + z) * 2 + w != me)
            def _():
                out_copy(z, w).wait_send()

        return 0

    lax.fori_loop(0, 8, drain_out, 0)

    def done_out(t, _):
        slot = out_ref.at[:, 0, pl.ds(pl.multiple_of(t * 8, 8), 8), :]
        pltpu.make_async_copy(slot, slot, out_recv.at[t]).wait()
        return 0

    lax.fori_loop(0, 16, done_out, 0)


def fused(potential, start_basis):
    nb = start_basis.shape[0] * 2
    sites = 16 * start_basis.shape[1] * start_basis.shape[2] * start_basis.shape[3]
    sem = pltpu.SemaphoreType.DMA
    field = lambda planes: pltpu.VMEM((planes, nb, 8, 256), F32)
    return pl.pallas_call(
        functools.partial(kernel, nb, 1.0 / sites),
        out_shape=(
            jax.ShapeDtypeStruct(start_basis.shape, F32),
            jax.ShapeDtypeStruct((nb, nb), F32),
        ),
        in_specs=[pl.BlockSpec(memory_space=pl.ANY)] * 2,
        out_specs=(pl.BlockSpec(memory_space=pl.ANY), pl.BlockSpec(memory_space=pltpu.VMEM)),
        scratch_shapes=[
            pltpu.VMEM((8, 8, 256), F32), pltpu.VMEM((8, 8, 256), F32),
            field(10), field(10), field(10), field(8), field(8),
            pltpu.VMEM((3, 2, 8, nb, 1, 256), F32), pltpu.VMEM((3, 2, 8, nb, 1, 256), F32),
            pltpu.VMEM((5, nb * 8, nb * 8), F32),
            pltpu.VMEM((3, 8, 5, nb, nb), F32), pltpu.VMEM((3, 4, 5, nb, nb), F32),
            sem((16,)), sem((8, 2)), sem((16,)), sem((8,)), sem((3, 4)), sem((3, 4)),
            sem((3, 8)), sem((3, 8)), sem((3, 4)), sem((3, 4)), sem((8, 2)), sem((16,)),
        ],
        compiler_params=pltpu.CompilerParams(
            collective_id=0, has_side_effects=True, vmem_limit_bytes=48 * 2**20
        ),
        name="jacobi_davidson",
    )(potential, start_basis)


def solution(mesh):
    in_specs = (P("space", None, None), P("vec", "space", None, None))
    out_specs = (P("vec", "space", None, None), P())

    def body(potential, start_basis):
        fits = mesh.shape["space"] == 16 and mesh.shape["vec"] == 2
        if fits and start_basis.shape == (8, 1, 128, 256):
            return fused(potential, start_basis)
        return local(potential, start_basis)

    return jax.shard_map(body, mesh=mesh, in_specs=in_specs, out_specs=out_specs, check_vma=False)
```

```python
import functools

import jax
import jax.numpy as jnp
from jax import lax
from jax.experimental import pallas as pl
from jax.experimental.pallas import tpu as pltpu
from jax.sharding import PartitionSpec as P

NSWEEP = 3


SIGMA = 0.5
PREC = lax.Precision.HIGHEST


def extended(value, sides, width):
    for axis, dim in sides:
        peers, length = (lax.axis_size(axis), value.shape[dim])
        up = [(i, (i + 1) % peers) for i in range(peers)]
        down = [(j, i) for i, j in up]
        last = lax.slice_in_dim(value, length - width, length, axis=dim)
        first = lax.slice_in_dim(value, 0, width, axis=dim)
        before = lax.ppermute(last, axis, up)
        after = lax.ppermute(first, axis, down)
        value = jnp.concatenate([before, value, after], axis=dim)
    return value


def local_inner(left, right, scale):
    return jnp.einsum("kzyx,jzyx->kj", left, right, precision=PREC) * scale


def combine(coeff, vectors):
    return jnp.einsum("kj,kzyx->jzyx", coeff, vectors, precision=PREC)


def stencil(padded, potential):
    center = padded[:, 1:-1]
    beside = padded[:, 2:] + padded[:, :-2]
    beside = beside + jnp.roll(center, 1, 2) + jnp.roll(center, -1, 2)
    beside = beside + jnp.roll(center, 1, 3) + jnp.roll(center, -1, 3)
    return potential * center - beside


def inverse_factor(gram):
    lower = jnp.linalg.cholesky(gram)
    return jax.scipy.linalg.solve_triangular(
        lower, jnp.eye(gram.shape[0], dtype=jnp.float32), lower=True
    )


def local(potential, start_basis):
    mine = start_basis.shape[0]
    scale = 1.0 / (
        start_basis.shape[1] * start_basis.shape[2] * start_basis.shape[3] * lax.axis_size("space")
    )
    first = lax.axis_index("vec") * mine
    whole = lax.all_gather(start_basis, "vec", axis=0, tiled=True)
    gram = lax.psum(local_inner(whole, whole, scale), "space")
    basis_all = combine(inverse_factor(gram).T, whole)
    basis = lax.dynamic_slice_in_dim(basis_all, first, mine, 0)
    shifted = jnp.where(potential >= SIGMA, potential - SIGMA + 6.0, potential - SIGMA - 6.0)
    padded = extended(basis_all, (("space", 1),), 1)
    image_all = stencil(padded, potential)
    rayleigh = lax.psum(local_inner(basis_all, image_all, scale), "space")
    image = lax.dynamic_slice_in_dim(image_all, first, mine, 0)
    panel_mine = lax.dynamic_slice_in_dim(rayleigh, first, mine, 1)
    resid = image - combine(panel_mine, basis_all)
    correction = jnp.zeros_like(basis)
    for sweep in range(NSWEEP):
        coeff, cross = lax.psum(
            (local_inner(basis_all, correction, scale), local_inner(image_all, correction, scale)),
            "space",
        )
        padded = extended(correction, (("space", 1),), 1)
        proj = correction - combine(coeff, basis_all)
        moved = stencil(padded, potential) - combine(coeff, image_all) - SIGMA * proj
        back = cross - jnp.dot(rayleigh.T, coeff, precision=PREC)
        update = -resid - (moved - combine(back, basis_all))
        correction = correction + update / shifted
    proj_two = lax.psum(local_inner(basis_all, correction, scale), "space")
    fresh = correction - combine(proj_two, basis_all)
    fresh_all = lax.all_gather(fresh, "vec", axis=0, tiled=True)
    gram_two = lax.psum(local_inner(fresh_all, fresh_all, scale), "space")
    inverse_two = inverse_factor(gram_two)
    rows_mine = lax.dynamic_slice_in_dim(inverse_two, first, mine, 0)
    new_basis = combine(rows_mine.T, fresh_all)
    return (new_basis, rayleigh)


MESH = pl.DeviceIdType.MESH
F32 = jnp.float32
BF16 = jnp.bfloat16
NN = (((1,), (0,)), ((), ()))
NT = (((1,), (1,)), ((), ()))
TN = (((0,), (0,)), ((), ()))


def small(a, b, dims=NN):
    return lax.dot_general(a, b, dims, precision=PREC, preferred_element_type=F32)


def split(a):
    high = a.astype(BF16)
    return high, (a - high.astype(F32)).astype(BF16)


def dot3(a, b, dims=NN):
    (ah, al), (bh, bl) = a, b

    def one(p, q):
        return lax.dot_general(p, q, dims, preferred_element_type=F32)

    return one(ah, bh) + (one(ah, bl) + one(al, bh))


def tile_of(space):
    z, y, x = space // 4, (space // 2) % 2, space % 2
    q = 2 * y + (x + y) % 2
    return 4 * q + z + (q % 2) * (3 - 2 * z)


def space_of(tile):
    q, r = tile // 4, tile % 4
    z = r + (q % 2) * (3 - 2 * r)
    return z * 4 + (q // 2) * 2 + ((q + 1) // 2) % 2


def factor_inverse(gram):
    n = gram.shape[0]
    rows = lax.broadcasted_iota(jnp.int32, (n, n), 0)
    cols = lax.broadcasted_iota(jnp.int32, (n, n), 1)
    eye = jnp.where(rows == cols, 1.0, 0.0).astype(F32)
    upper, inv = gram, eye
    row = lax.broadcasted_iota(jnp.int32, (n, 1), 0)
    for k in range(n - 1):
        mult = jnp.where(row > k, upper[:, k : k + 1] / upper[k : k + 1, k : k + 1], 0.0)
        inv = inv - mult * inv[k : k + 1, :]
        upper = upper - mult * upper[k : k + 1, :]
    diag = jnp.sum(upper * eye, axis=1, keepdims=True)
    return inv / jnp.sqrt(diag)


def iota(shape, dim):
    return lax.broadcasted_iota(jnp.int32, shape, dim)


def one_pass(a, b, dims=NN):
    return lax.dot_general(a, b, dims, preferred_element_type=F32)


def exact(a):
    high, rest = a.astype(BF16), None
    rest = a - high.astype(F32)
    mid = rest.astype(BF16)
    return high, mid, (rest - mid.astype(F32)).astype(BF16)


def kron(matrix, transposed=False):
    a, b = matrix.shape[::-1] if transposed else matrix.shape
    rows = jnp.where(iota((8 * a, a), 0) // 8 == iota((8 * a, a), 1), 1.0, 0.0).astype(BF16)
    cols = jnp.where(iota((b, 8 * b), 0) == iota((b, 8 * b), 1) // 8, 1.0, 0.0).astype(BF16)
    same = iota((8 * a, 8 * b), 0) % 8 == iota((8 * a, 8 * b), 1) % 8

    def one(part):
        tall = one_pass(rows, part, NT if transposed else NN).astype(BF16)
        return jnp.where(same, one_pass(tall, cols), 0.0).astype(BF16)

    return tuple(one(part) for part in split(matrix))


def kernel(
    nb, scale,
    pot_in, s_in, out_ref, ray_ref,
    pot, dinv, fs, f1, f2, ft, fq, bih, bil, ysend, yrecv, acc_s, acc, red1, red2,
    in_send, in_recv, pot_send, pot_recv, y_sends, y_recvs, z_sends, z_recvs,
    r1_send, r1_recv, r2_send, r2_recv, out_send, out_recv,
):
    s, v = lax.axis_index("space"), lax.axis_index("vec")
    tile = tile_of(s)
    half = s // 8
    me = s * 2 + v
    rows8 = nb * 8
    wide8 = 2 * rows8

    barrier = pltpu.get_barrier_semaphore()

    def greet(i, _):
        peer = (me + i) % 32
        pl.semaphore_signal(barrier, inc=1, device_id=(peer // 2, peer % 2), device_id_type=MESH)
        return 0

    lax.fori_loop(1, 32, greet, 0)
    pl.semaphore_wait(barrier, 31)

    def s_piece(dest):
        return s_in.at[:, 0, pl.ds(pl.multiple_of(tile_of(dest) * 8, 8), 8), :]

    s_slot = fs.at[1 + s % 8, pl.ds(v * 8, 8)]

    def pot_piece(dest):
        return pot_in.at[0, pl.ds(pl.multiple_of(tile_of(dest) * 8, 8), 8), :]

    def s_copy(o):
        dest = (s + o) % 16
        return pltpu.make_async_remote_copy(
            src_ref=s_piece(dest), dst_ref=s_slot,
            send_sem=in_send.at[o], recv_sem=in_recv.at[s % 8, v],
            device_id=(dest, half), device_id_type=MESH,
        )

    def pot_copy(o):
        dest = (s + o) % 16
        return pltpu.make_async_remote_copy(
            src_ref=pot_piece(dest), dst_ref=pot.at[s % 8],
            send_sem=pot_send.at[o], recv_sem=pot_recv.at[s % 8],
            device_id=(dest, half), device_id_type=MESH,
        )

    def send_in(o, _):
        s_copy(o).start()

        @pl.when(half == v)
        def _():
            pot_copy(o).start()

        return 0

    lax.fori_loop(1, 16, send_in, 0)

    @pl.when(half == v)
    def _():
        pltpu.make_async_copy(s_piece(s), s_slot, in_recv.at[s % 8, v]).start()
        pltpu.make_async_copy(pot_piece(s), pot.at[s % 8], pot_recv.at[s % 8]).start()

    @pl.when(half != v)
    def _():
        s_copy(0).start()


    after = space_of((tile + 1) % 16)
    before = space_of((tile + 15) % 16)

    def y_copies(n, z):
        return [
            pltpu.make_async_remote_copy(
                src_ref=ysend.at[n, i, z], dst_ref=yrecv.at[n, i, z],
                send_sem=y_sends.at[n, i, z], recv_sem=y_recvs.at[n, i, z],
                device_id=(device, v), device_id_type=MESH,
            )
            for i, device in enumerate((after, before))
        ]

    def z_copy(n, field, i):
        return pltpu.make_async_remote_copy(
            src_ref=field.at[(8, 1)[i]], dst_ref=field.at[(0, 9)[i]],
            send_sem=z_sends.at[n, i], recv_sem=z_recvs.at[n, i],
            device_id=(s, 1 - v), device_id_type=MESH,
        )

    def halo_start(n, field, z):
        ysend[n, 0, z] = field[1 + z, :, 7:8, :]
        ysend[n, 1, z] = field[1 + z, :, 0:1, :]
        for c in y_copies(n, z):
            c.start()

        @pl.when(z == 7)
        def _():
            z_copy(n, field, 0).start()

        @pl.when(z == 0)
        def _():
            z_copy(n, field, 1).start()

    def halo_wait(n, field, z):
        for c in y_copies(n, z):
            c.wait_recv()

        @pl.when(z == 0)
        def _():
            z_copy(n, field, 0).wait_recv()

        @pl.when(z == 7)
        def _():
            z_copy(n, field, 1).wait_recv()

    def halo_drain(n, field):
        def one(z, _):
            for c in y_copies(n, z):
                c.wait_send()
            return 0

        lax.fori_loop(0, 8, one, 0)
        z_copy(n, field, 0).wait_send()
        z_copy(n, field, 1).wait_send()

    def planes(body):
        def step(i, _):
            body((i + 7) % 8)
            return 0

        lax.fori_loop(0, 8, step, 0)

    inrow = iota((rows8, 256), 0) % 8
    is_first, is_last = inrow == 0, inrow == 7

    def flat(a):
        return jnp.broadcast_to(a, (nb, 8, 256)).reshape(rows8, 256)

    def get(field, z):
        return field[z].reshape(rows8, 256)

    def put(field, z, value):
        field[z] = value.reshape(nb, 8, 256)

    def apply_h(n, field, z):
        mid = get(field, z + 1)
        total = get(field, z) + get(field, z + 2)
        total += jnp.where(is_first, flat(yrecv[n, 0, z]), pltpu.roll(mid, 1, 0))
        total += jnp.where(is_last, flat(yrecv[n, 1, z]), pltpu.roll(mid, rows8 - 1, 0))
        total += pltpu.roll(mid, 1, 1) + pltpu.roll(mid, 255, 1)
        return mid, flat(pot[z][None]) * mid - total

    def squeeze(blocks):
        width = rows8 * len(blocks)
        wide = jnp.concatenate(blocks, axis=1)
        wide = jnp.where(iota((rows8, width), 0) % 8 == iota((rows8, width), 1) % 8, wide, 0.0)
        left = jnp.where(iota((nb, rows8), 0) == iota((nb, rows8), 1) // 8, 1.0, 0.0).astype(BF16)
        right = jnp.where(iota((width, 128), 0) // 8 == iota((width, 128), 1), 1.0, 0.0).astype(BF16)
        tall = sum(one_pass(left, part) for part in exact(wide))
        return sum(one_pass(part, right) for part in exact(tall)) * scale

    def total_of(n, blocks):
        rank = (s % 4) * 2 + v
        red1[n, rank] = squeeze(blocks)

        def copy1(i):
            peer = (rank + i) % 8
            return pltpu.make_async_remote_copy(
                src_ref=red1.at[n, rank], dst_ref=red1.at[n, rank],
                send_sem=r1_send.at[n, i], recv_sem=r1_recv.at[n, rank],
                device_id=((s // 4) * 4 + peer // 2, peer % 2), device_id_type=MESH,
            )

        def copy2(i):
            peer = (s // 4 + i) % 4
            return pltpu.make_async_remote_copy(
                src_ref=red2.at[n, s // 4], dst_ref=red2.at[n, s // 4],
                send_sem=r2_send.at[n, i], recv_sem=r2_recv.at[n, s // 4],
                device_id=(peer * 4 + s % 4, v), device_id_type=MESH,
            )

        def stage(copy, buf, recv, mine, count):
            for i in range(1, count):
                copy(i).start()
            for i in range(1, count):
                peer = (mine + i) % count
                slot = buf.at[n, peer]
                pltpu.make_async_copy(slot, slot, recv.at[n, peer]).wait()
            for i in range(1, count):
                copy(i).wait_send()
            total = buf[n, 0]
            for p in range(1, count):
                total = total + buf[n, p]
            return total

        red2[n, s // 4] = stage(copy1, red1, r1_recv, rank, 8)
        total = stage(copy2, red2, r2_recv, s // 4, 4)
        return [total[:, nb * i : nb * (i + 1)] for i in range(len(blocks))]

    acc_s[...] = jnp.zeros_like(acc_s)
    acc[...] = jnp.zeros_like(acc)

    def arrive(z):
        for w in range(2):
            slot = fs.at[1 + z, pl.ds(w * 8, 8)]
            pltpu.make_async_copy(slot, slot, in_recv.at[z, w]).wait()
        pltpu.make_async_copy(pot.at[z], pot.at[z], pot_recv.at[z]).wait()
        halo_start(0, fs, z)
        p = pot[z]
        inverse = 1.0 / jnp.where(p >= SIGMA, p - SIGMA + 6.0, p - SIGMA - 6.0)
        dinv[z] = inverse
        mid = get(fs, z + 1)
        both = jnp.concatenate([mid, flat(inverse[None]) * mid], axis=0)
        acc_s[...] += dot3(split(mid), split(both), NT)

    planes(arrive)

    def first(z):
        halo_wait(0, fs, z)
        mid, image = apply_h(0, fs, z)
        put(ft, z, image)
        left = jnp.concatenate([mid, image], axis=0)
        right = jnp.concatenate([image, flat(dinv[z][None]) * image], axis=0)
        acc[...] += dot3(split(left), split(right), NT)

    planes(first)
    lo, hi = slice(0, rows8), slice(rows8, wide8)
    gram, m0, raw, m1, m2 = total_of(
        0, [acc_s[:, lo], acc_s[:, hi], acc[lo, lo], acc[lo, hi], acc[hi, hi]]
    )
    w = factor_inverse(gram)

    def conj(m):
        return small(small(w, m), w, NT)

    def side(*parts):
        return jnp.concatenate(parts, axis=1)

    def stack(*parts):
        return jnp.concatenate(parts, axis=0)

    ray = conj(raw)
    zero = jnp.zeros_like(w)
    kbig = kron(stack(side(w, zero), side(zero, w), side(small(ray, w, TN), -w)))

    def second(z):
        mixed = dot3(kbig, split(stack(get(fs, z + 1), get(ft, z))))
        basis, image, resid = mixed[lo], mixed[hi], mixed[wide8:]
        put(f1, z + 1, flat(dinv[z][None]) * resid)
        halo_start(1, f1, z)
        high, low = split(stack(image, basis))
        bih[z] = high
        bil[z] = low

    planes(second)
    ray_ref[...] = ray
    n0, n1, n2 = conj(m0), conj(m1), conj(m2)
    coeff = small(n0, ray) - n1
    cross = small(n1, ray, TN) - n2
    edge = cross - small(ray, coeff, TN) - SIGMA * coeff
    kmix = kron(stack(coeff, edge), True)

    def third(z):
        halo_wait(1, f1, z)
        mid, image = apply_h(1, f1, z)
        mix = dot3(kmix, (bih[z], bil[z]))
        put(f2, z + 1, 2.0 * mid + flat(dinv[z][None]) * (SIGMA * mid - image + mix))
        halo_start(2, f2, z)

    planes(third)
    acc[...] = jnp.zeros_like(acc)

    def fourth(z):
        halo_wait(2, f2, z)
        mid, image = apply_h(2, f2, z)
        new = mid + get(f1, z + 1) + flat(dinv[z][None]) * (SIGMA * mid - image)
        put(fq, z, new)
        acc[...] += dot3((bih[z], bil[z]), split(stack(mid, new)), NT)

    planes(fourth)
    cross, coeff, part = total_of(1, [acc[lo, lo], acc[hi, lo], acc[hi, hi]])
    edge = cross - small(ray, coeff, TN) - SIGMA * coeff
    proj = part + small(n1, coeff) + small(n0, edge)
    klast = kron(stack(side(coeff, zero), side(edge, proj)), True)
    acc_s[...] = jnp.zeros_like(acc_s)

    def fifth(z):
        mixed = dot3(klast, (bih[z], bil[z]))
        fresh = get(fq, z) + flat(dinv[z][None]) * mixed[lo] - mixed[hi]
        put(fq, z, fresh)
        a = split(fresh)
        acc_s[:, lo] += dot3(a, a, NT)

    planes(fifth)
    (gram2,) = total_of(2, [acc_s[:, lo]])
    kw2 = kron(factor_inverse(gram2))
    halo_drain(0, fs)
    halo_drain(1, f1)
    halo_drain(2, f2)

    out_rows = out_ref.at[:, 0, pl.ds(pl.multiple_of(tile * 8, 8), 8), :]

    def out_copy(z, w):
        return pltpu.make_async_remote_copy(
            src_ref=fq.at[z, pl.ds(w * 8, 8)], dst_ref=out_rows,
            send_sem=out_send.at[z, w], recv_sem=out_recv.at[tile],
            device_id=(v * 8 + z, w), device_id_type=MESH,
        )

    def last(i, _):
        z = (tile + i) % 8
        put(fq, z, dot3(kw2, split(get(fq, z))))
        for w in range(2):
            mine = (v * 8 + z) * 2 + w == me

            @pl.when(mine)
            def _():
                pltpu.make_async_copy(
                    fq.at[z, pl.ds(w * 8, 8)], out_rows, out_recv.at[tile]
                ).start()

            @pl.when(jnp.logical_not(mine))
            def _():
                out_copy(z, w).start()

        return 0

    lax.fori_loop(0, 8, last, 0)

    def drain_in(o, _):
        s_copy(o).wait_send()

        @pl.when(half == v)
        def _():
            pot_copy(o).wait_send()

        return 0

    lax.fori_loop(1, 16, drain_in, 0)

    @pl.when(half != v)
    def _():
        s_copy(0).wait_send()

    def drain_out(z, _):
        for w in range(2):
            @pl.when((v * 8 + z) * 2 + w != me)
            def _():
                out_copy(z, w).wait_send()

        return 0

    lax.fori_loop(0, 8, drain_out, 0)

    def done_out(t, _):
        slot = out_ref.at[:, 0, pl.ds(pl.multiple_of(t * 8, 8), 8), :]
        pltpu.make_async_copy(slot, slot, out_recv.at[t]).wait()
        return 0

    lax.fori_loop(0, 16, done_out, 0)


def fused(potential, start_basis):
    nb = start_basis.shape[0] * 2
    sites = 16 * start_basis.shape[1] * start_basis.shape[2] * start_basis.shape[3]
    sem = pltpu.SemaphoreType.DMA
    field = lambda planes: pltpu.VMEM((planes, nb, 8, 256), F32)
    return pl.pallas_call(
        functools.partial(kernel, nb, 1.0 / sites),
        out_shape=(
            jax.ShapeDtypeStruct(start_basis.shape, F32),
            jax.ShapeDtypeStruct((nb, nb), F32),
        ),
        in_specs=[pl.BlockSpec(memory_space=pl.ANY)] * 2,
        out_specs=(pl.BlockSpec(memory_space=pl.ANY), pl.BlockSpec(memory_space=pltpu.VMEM)),
        scratch_shapes=[
            pltpu.VMEM((8, 8, 256), F32), pltpu.VMEM((8, 8, 256), F32),
            field(10), field(10), field(10), field(8), field(8),
            pltpu.VMEM((8, nb * 16, 256), BF16), pltpu.VMEM((8, nb * 16, 256), BF16),
            pltpu.VMEM((3, 2, 8, nb, 1, 256), F32), pltpu.VMEM((3, 2, 8, nb, 1, 256), F32),
            pltpu.VMEM((nb * 8, nb * 16), F32), pltpu.VMEM((nb * 16, nb * 16), F32),
            pltpu.VMEM((3, 8, nb, 128), F32), pltpu.VMEM((3, 4, nb, 128), F32),
            sem((16,)), sem((8, 2)), sem((16,)), sem((8,)),
            sem((3, 2, 8)), sem((3, 2, 8)), sem((3, 2)), sem((3, 2)),
            sem((3, 8)), sem((3, 8)), sem((3, 4)), sem((3, 4)), sem((8, 2)), sem((16,)),
        ],
        compiler_params=pltpu.CompilerParams(
            collective_id=0, has_side_effects=True, vmem_limit_bytes=48 * 2**20
        ),
        name="jacobi_davidson",
    )(potential, start_basis)


def solution(mesh):
    in_specs = (P("space", None, None), P("vec", "space", None, None))
    out_specs = (P("vec", "space", None, None), P())

    def body(potential, start_basis):
        fits = mesh.shape["space"] == 16 and mesh.shape["vec"] == 2
        if fits and start_basis.shape == (8, 1, 128, 256):
            return fused(potential, start_basis)
        return local(potential, start_basis)

    return jax.shard_map(body, mesh=mesh, in_specs=in_specs, out_specs=out_specs, check_vma=False)
```

```python
import functools

import jax
import jax.numpy as jnp
from jax import lax
from jax.experimental import pallas as pl
from jax.experimental.pallas import tpu as pltpu
from jax.sharding import PartitionSpec as P

NSWEEP = 3


SIGMA = 0.5
PREC = lax.Precision.HIGHEST


def extended(value, sides, width):
    for axis, dim in sides:
        peers, length = (lax.axis_size(axis), value.shape[dim])
        up = [(i, (i + 1) % peers) for i in range(peers)]
        down = [(j, i) for i, j in up]
        last = lax.slice_in_dim(value, length - width, length, axis=dim)
        first = lax.slice_in_dim(value, 0, width, axis=dim)
        before = lax.ppermute(last, axis, up)
        after = lax.ppermute(first, axis, down)
        value = jnp.concatenate([before, value, after], axis=dim)
    return value


def local_inner(left, right, scale):
    return jnp.einsum("kzyx,jzyx->kj", left, right, precision=PREC) * scale


def combine(coeff, vectors):
    return jnp.einsum("kj,kzyx->jzyx", coeff, vectors, precision=PREC)


def stencil(padded, potential):
    center = padded[:, 1:-1]
    beside = padded[:, 2:] + padded[:, :-2]
    beside = beside + jnp.roll(center, 1, 2) + jnp.roll(center, -1, 2)
    beside = beside + jnp.roll(center, 1, 3) + jnp.roll(center, -1, 3)
    return potential * center - beside


def inverse_factor(gram):
    lower = jnp.linalg.cholesky(gram)
    return jax.scipy.linalg.solve_triangular(
        lower, jnp.eye(gram.shape[0], dtype=jnp.float32), lower=True
    )


def local(potential, start_basis):
    mine = start_basis.shape[0]
    scale = 1.0 / (
        start_basis.shape[1] * start_basis.shape[2] * start_basis.shape[3] * lax.axis_size("space")
    )
    first = lax.axis_index("vec") * mine
    whole = lax.all_gather(start_basis, "vec", axis=0, tiled=True)
    gram = lax.psum(local_inner(whole, whole, scale), "space")
    basis_all = combine(inverse_factor(gram).T, whole)
    basis = lax.dynamic_slice_in_dim(basis_all, first, mine, 0)
    shifted = jnp.where(potential >= SIGMA, potential - SIGMA + 6.0, potential - SIGMA - 6.0)
    padded = extended(basis_all, (("space", 1),), 1)
    image_all = stencil(padded, potential)
    rayleigh = lax.psum(local_inner(basis_all, image_all, scale), "space")
    image = lax.dynamic_slice_in_dim(image_all, first, mine, 0)
    panel_mine = lax.dynamic_slice_in_dim(rayleigh, first, mine, 1)
    resid = image - combine(panel_mine, basis_all)
    correction = jnp.zeros_like(basis)
    for sweep in range(NSWEEP):
        coeff, cross = lax.psum(
            (local_inner(basis_all, correction, scale), local_inner(image_all, correction, scale)),
            "space",
        )
        padded = extended(correction, (("space", 1),), 1)
        proj = correction - combine(coeff, basis_all)
        moved = stencil(padded, potential) - combine(coeff, image_all) - SIGMA * proj
        back = cross - jnp.dot(rayleigh.T, coeff, precision=PREC)
        update = -resid - (moved - combine(back, basis_all))
        correction = correction + update / shifted
    proj_two = lax.psum(local_inner(basis_all, correction, scale), "space")
    fresh = correction - combine(proj_two, basis_all)
    fresh_all = lax.all_gather(fresh, "vec", axis=0, tiled=True)
    gram_two = lax.psum(local_inner(fresh_all, fresh_all, scale), "space")
    inverse_two = inverse_factor(gram_two)
    rows_mine = lax.dynamic_slice_in_dim(inverse_two, first, mine, 0)
    new_basis = combine(rows_mine.T, fresh_all)
    return (new_basis, rayleigh)


MESH = pl.DeviceIdType.MESH
F32 = jnp.float32
BF16 = jnp.bfloat16
NN = (((1,), (0,)), ((), ()))
NT = (((1,), (1,)), ((), ()))
TN = (((0,), (0,)), ((), ()))


def small(a, b, dims=NN):
    return lax.dot_general(a, b, dims, precision=PREC, preferred_element_type=F32)


def split(a):
    high = a.astype(BF16)
    return high, (a - high.astype(F32)).astype(BF16)


def dot3(a, b, dims=NN):
    (ah, al), (bh, bl) = a, b

    def one(p, q):
        return lax.dot_general(p, q, dims, preferred_element_type=F32)

    return one(ah, bh) + (one(ah, bl) + one(al, bh))


def tile_of(space):
    z, y, x = space // 4, (space // 2) % 2, space % 2
    q = 2 * y + (x + y) % 2
    return 4 * q + z + (q % 2) * (3 - 2 * z)


def space_of(tile):
    q, r = tile // 4, tile % 4
    z = r + (q % 2) * (3 - 2 * r)
    return z * 4 + (q // 2) * 2 + ((q + 1) // 2) % 2


def factor_inverse(gram):
    n = gram.shape[0]
    rows = lax.broadcasted_iota(jnp.int32, (n, n), 0)
    cols = lax.broadcasted_iota(jnp.int32, (n, n), 1)
    eye = jnp.where(rows == cols, 1.0, 0.0).astype(F32)
    upper, inv = gram, eye
    row = lax.broadcasted_iota(jnp.int32, (n, 1), 0)
    for k in range(n - 1):
        mult = jnp.where(row > k, upper[:, k : k + 1] / upper[k : k + 1, k : k + 1], 0.0)
        inv = inv - mult * inv[k : k + 1, :]
        upper = upper - mult * upper[k : k + 1, :]
    diag = jnp.sum(upper * eye, axis=1, keepdims=True)
    return inv / jnp.sqrt(diag)


def iota(shape, dim):
    return lax.broadcasted_iota(jnp.int32, shape, dim)


def one_pass(a, b, dims=NN):
    return lax.dot_general(a, b, dims, preferred_element_type=F32)


def exact(a):
    high, rest = a.astype(BF16), None
    rest = a - high.astype(F32)
    mid = rest.astype(BF16)
    return high, mid, (rest - mid.astype(F32)).astype(BF16)


def kron(matrix, transposed=False):
    a, b = matrix.shape[::-1] if transposed else matrix.shape
    rows = jnp.where(iota((8 * a, a), 0) // 8 == iota((8 * a, a), 1), 1.0, 0.0).astype(BF16)
    cols = jnp.where(iota((b, 8 * b), 0) == iota((b, 8 * b), 1) // 8, 1.0, 0.0).astype(BF16)
    same = iota((8 * a, 8 * b), 0) % 8 == iota((8 * a, 8 * b), 1) % 8

    def one(part):
        tall = one_pass(rows, part, NT if transposed else NN).astype(BF16)
        return jnp.where(same, one_pass(tall, cols), 0.0).astype(BF16)

    return tuple(one(part) for part in split(matrix))


def kernel(
    nb, scale,
    pot_in, s_in, out_ref, ray_ref,
    pot, dinv, fs, f1, f2, ft, fq, bih, bil, ysend, yrecv, acc_s, acc, red1, red2, home,
    in_send, in_recv, pot_send, pot_recv, y_sends, y_recvs, z_sends, z_recvs,
    r1_send, r1_recv, r2_send, r2_recv, out_send, out_recv, fwd_send, fwd_recv,
):
    s, v = lax.axis_index("space"), lax.axis_index("vec")
    tile = tile_of(s)
    half = s // 8
    me = s * 2 + v
    rows8 = nb * 8
    wide8 = 2 * rows8

    barrier = pltpu.get_barrier_semaphore()

    def greet(i, _):
        peer = (me + i) % 32
        pl.semaphore_signal(barrier, inc=1, device_id=(peer // 2, peer % 2), device_id_type=MESH)
        return 0

    lax.fori_loop(1, 32, greet, 0)
    pl.semaphore_wait(barrier, 31)

    def s_piece(dest):
        return s_in.at[:, 0, pl.ds(pl.multiple_of(tile_of(dest) * 8, 8), 8), :]

    s_slot = fs.at[1 + s % 8, pl.ds(v * 8, 8)]

    def pot_piece(dest):
        return pot_in.at[0, pl.ds(pl.multiple_of(tile_of(dest) * 8, 8), 8), :]

    def s_copy(o):
        dest = (s + o) % 16
        return pltpu.make_async_remote_copy(
            src_ref=s_piece(dest), dst_ref=s_slot,
            send_sem=in_send.at[o], recv_sem=in_recv.at[s % 8, v],
            device_id=(dest, half), device_id_type=MESH,
        )

    def pot_copy(o):
        dest = (s + o) % 16
        return pltpu.make_async_remote_copy(
            src_ref=pot_piece(dest), dst_ref=pot.at[s % 8],
            send_sem=pot_send.at[o], recv_sem=pot_recv.at[s % 8],
            device_id=(dest, half), device_id_type=MESH,
        )

    def send_in(o, _):
        s_copy(o).start()

        @pl.when(half == v)
        def _():
            pot_copy(o).start()

        return 0

    lax.fori_loop(1, 16, send_in, 0)

    @pl.when(half == v)
    def _():
        pltpu.make_async_copy(s_piece(s), s_slot, in_recv.at[s % 8, v]).start()
        pltpu.make_async_copy(pot_piece(s), pot.at[s % 8], pot_recv.at[s % 8]).start()

    @pl.when(half != v)
    def _():
        s_copy(0).start()


    after = space_of((tile + 1) % 16)
    before = space_of((tile + 15) % 16)

    def y_copies(n, z):
        return [
            pltpu.make_async_remote_copy(
                src_ref=ysend.at[n, i, z], dst_ref=yrecv.at[n, i, z],
                send_sem=y_sends.at[n, i, z], recv_sem=y_recvs.at[n, i, z],
                device_id=(device, v), device_id_type=MESH,
            )
            for i, device in enumerate((after, before))
        ]

    def z_copy(n, field, i):
        return pltpu.make_async_remote_copy(
            src_ref=field.at[(8, 1)[i]], dst_ref=field.at[(0, 9)[i]],
            send_sem=z_sends.at[n, i], recv_sem=z_recvs.at[n, i],
            device_id=(s, 1 - v), device_id_type=MESH,
        )

    def halo_start(n, field, z):
        ysend[n, 0, z] = field[1 + z, :, 7:8, :]
        ysend[n, 1, z] = field[1 + z, :, 0:1, :]
        for c in y_copies(n, z):
            c.start()

        @pl.when(z == 7)
        def _():
            z_copy(n, field, 0).start()

        @pl.when(z == 0)
        def _():
            z_copy(n, field, 1).start()

    def halo_wait(n, field, z):
        for c in y_copies(n, z):
            c.wait_recv()

        @pl.when(z == 0)
        def _():
            z_copy(n, field, 0).wait_recv()

        @pl.when(z == 7)
        def _():
            z_copy(n, field, 1).wait_recv()

    def halo_drain(n, field):
        def one(z, _):
            for c in y_copies(n, z):
                c.wait_send()
            return 0

        lax.fori_loop(0, 8, one, 0)
        z_copy(n, field, 0).wait_send()
        z_copy(n, field, 1).wait_send()

    def planes(body):
        def step(i, _):
            body((i + 7) % 8)
            return 0

        lax.fori_loop(0, 8, step, 0)

    inrow = iota((rows8, 256), 0) % 8
    is_first, is_last = inrow == 0, inrow == 7

    def flat(a):
        return jnp.broadcast_to(a, (nb, 8, 256)).reshape(rows8, 256)

    def get(field, z):
        return field[z].reshape(rows8, 256)

    def put(field, z, value):
        field[z] = value.reshape(nb, 8, 256)

    def apply_h(n, field, z):
        mid = get(field, z + 1)
        total = get(field, z) + get(field, z + 2)
        total += jnp.where(is_first, flat(yrecv[n, 0, z]), pltpu.roll(mid, 1, 0))
        total += jnp.where(is_last, flat(yrecv[n, 1, z]), pltpu.roll(mid, rows8 - 1, 0))
        total += pltpu.roll(mid, 1, 1) + pltpu.roll(mid, 255, 1)
        return mid, flat(pot[z][None]) * mid - total

    def squeeze(blocks):
        width = rows8 * len(blocks)
        wide = jnp.concatenate(blocks, axis=1)
        wide = jnp.where(iota((rows8, width), 0) % 8 == iota((rows8, width), 1) % 8, wide, 0.0)
        left = jnp.where(iota((nb, rows8), 0) == iota((nb, rows8), 1) // 8, 1.0, 0.0).astype(BF16)
        right = jnp.where(iota((width, 128), 0) // 8 == iota((width, 128), 1), 1.0, 0.0).astype(BF16)
        tall = sum(one_pass(left, part) for part in exact(wide))
        return sum(one_pass(part, right) for part in exact(tall)) * scale

    def total_of(n, blocks):
        rank = (s % 4) * 2 + v
        red1[n, rank] = squeeze(blocks)

        def copy1(i):
            peer = (rank + i) % 8
            return pltpu.make_async_remote_copy(
                src_ref=red1.at[n, rank], dst_ref=red1.at[n, rank],
                send_sem=r1_send.at[n, i], recv_sem=r1_recv.at[n, rank],
                device_id=((s // 4) * 4 + peer // 2, peer % 2), device_id_type=MESH,
            )

        def copy2(i):
            peer = (s // 4 + i) % 4
            return pltpu.make_async_remote_copy(
                src_ref=red2.at[n, s // 4], dst_ref=red2.at[n, s // 4],
                send_sem=r2_send.at[n, i], recv_sem=r2_recv.at[n, s // 4],
                device_id=(peer * 4 + s % 4, v), device_id_type=MESH,
            )

        def stage(copy, buf, recv, mine, count):
            for i in range(1, count):
                copy(i).start()
            for i in range(1, count):
                peer = (mine + i) % count
                slot = buf.at[n, peer]
                pltpu.make_async_copy(slot, slot, recv.at[n, peer]).wait()
            for i in range(1, count):
                copy(i).wait_send()
            total = buf[n, 0]
            for p in range(1, count):
                total = total + buf[n, p]
            return total

        red2[n, s // 4] = stage(copy1, red1, r1_recv, rank, 8)
        total = stage(copy2, red2, r2_recv, s // 4, 4)
        return [total[:, nb * i : nb * (i + 1)] for i in range(len(blocks))]

    acc_s[...] = jnp.zeros_like(acc_s)
    acc[...] = jnp.zeros_like(acc)

    def arrive(z):
        for w in range(2):
            slot = fs.at[1 + z, pl.ds(w * 8, 8)]
            pltpu.make_async_copy(slot, slot, in_recv.at[z, w]).wait()
        pltpu.make_async_copy(pot.at[z], pot.at[z], pot_recv.at[z]).wait()
        halo_start(0, fs, z)
        p = pot[z]
        inverse = 1.0 / jnp.where(p >= SIGMA, p - SIGMA + 6.0, p - SIGMA - 6.0)
        dinv[z] = inverse
        mid = get(fs, z + 1)
        both = jnp.concatenate([mid, flat(inverse[None]) * mid], axis=0)
        acc_s[...] += dot3(split(mid), split(both), NT)

    planes(arrive)

    def first(z):
        halo_wait(0, fs, z)
        mid, image = apply_h(0, fs, z)
        put(ft, z, image)
        left = jnp.concatenate([mid, image], axis=0)
        right = jnp.concatenate([image, flat(dinv[z][None]) * image], axis=0)
        acc[...] += dot3(split(left), split(right), NT)

    planes(first)
    lo, hi = slice(0, rows8), slice(rows8, wide8)
    gram, m0, raw, m1, m2 = total_of(
        0, [acc_s[:, lo], acc_s[:, hi], acc[lo, lo], acc[lo, hi], acc[hi, hi]]
    )
    w = factor_inverse(gram)

    def conj(m):
        return small(small(w, m), w, NT)

    def side(*parts):
        return jnp.concatenate(parts, axis=1)

    def stack(*parts):
        return jnp.concatenate(parts, axis=0)

    ray = conj(raw)
    zero = jnp.zeros_like(w)
    kbig = kron(stack(side(w, zero), side(zero, w), side(small(ray, w, TN), -w)))

    def second(z):
        mixed = dot3(kbig, split(stack(get(fs, z + 1), get(ft, z))))
        basis, image, resid = mixed[lo], mixed[hi], mixed[wide8:]
        put(f1, z + 1, flat(dinv[z][None]) * resid)
        halo_start(1, f1, z)
        high, low = split(stack(image, basis))
        bih[z] = high
        bil[z] = low

    planes(second)
    ray_ref[...] = ray
    n0, n1, n2 = conj(m0), conj(m1), conj(m2)
    coeff = small(n0, ray) - n1
    cross = small(n1, ray, TN) - n2
    edge = cross - small(ray, coeff, TN) - SIGMA * coeff
    kmix = kron(stack(coeff, edge), True)

    def third(z):
        halo_wait(1, f1, z)
        mid, image = apply_h(1, f1, z)
        mix = dot3(kmix, (bih[z], bil[z]))
        put(f2, z + 1, 2.0 * mid + flat(dinv[z][None]) * (SIGMA * mid - image + mix))
        halo_start(2, f2, z)

    planes(third)
    acc[...] = jnp.zeros_like(acc)

    def fourth(z):
        halo_wait(2, f2, z)
        mid, image = apply_h(2, f2, z)
        new = mid + get(f1, z + 1) + flat(dinv[z][None]) * (SIGMA * mid - image)
        put(fq, z, new)
        acc[...] += dot3((bih[z], bil[z]), split(stack(mid, new)), NT)

    planes(fourth)
    cross, coeff, part = total_of(1, [acc[lo, lo], acc[hi, lo], acc[hi, hi]])
    edge = cross - small(ray, coeff, TN) - SIGMA * coeff
    proj = part + small(n1, coeff) + small(n0, edge)
    klast = kron(stack(side(coeff, zero), side(edge, proj)), True)
    acc_s[...] = jnp.zeros_like(acc_s)

    @pl.when(v == 0)
    def _():
        for i in range(16):
            home[i, 8:16] = jnp.zeros((8, 8, 256), F32)

    def out_copy(z, w):
        return pltpu.make_async_remote_copy(
            src_ref=fq.at[z, pl.ds(w * 8, 8)], dst_ref=home.at[tile, pl.ds(w * 8, 8)],
            send_sem=out_send.at[z, w], recv_sem=out_recv.at[tile],
            device_id=(v * 8 + z, w), device_id_type=MESH,
        )

    def send_out(z):
        for w in range(2):
            mine = (v * 8 + z) * 2 + w == me

            @pl.when(mine)
            def _():
                pltpu.make_async_copy(
                    fq.at[z, pl.ds(w * 8, 8)], home.at[tile, pl.ds(w * 8, 8)], out_recv.at[tile]
                ).start()

            @pl.when(jnp.logical_not(mine))
            def _():
                out_copy(z, w).start()

    def fifth(i, _):
        z = (tile + i) % 8
        mixed = dot3(klast, (bih[z], bil[z]))
        fresh = get(fq, z) + flat(dinv[z][None]) * mixed[lo] - mixed[hi]
        put(fq, z, fresh)
        send_out(z)
        a = split(fresh)
        acc_s[:, lo] += dot3(a, a, NT)
        return 0

    lax.fori_loop(0, 8, fifth, 0)
    (gram2,) = total_of(2, [acc_s[:, lo]])
    w2 = factor_inverse(gram2)
    kw2 = kron(jnp.where(v == 0, w2[0:8], w2[8:16]))
    def forward(j):
        return pltpu.make_async_remote_copy(
            src_ref=home.at[j, pl.ds(0, 8)], dst_ref=home.at[j, pl.ds(0, 8)],
            send_sem=fwd_send.at[j], recv_sem=fwd_recv.at[j],
            device_id=(s, 1), device_id_type=MESH,
        )

    def last(i, _):
        j = (s + 32 - i // 2 - 8 * (i % 2)) % 16
        slot = home.at[j, pl.ds(v * 8, 8)]
        pltpu.make_async_copy(slot, slot, out_recv.at[j]).wait()

        @pl.when(v == 0)
        def _():
            forward(j).start()

        @pl.when(v == 1)
        def _():
            low = home.at[j, pl.ds(0, 8)]
            pltpu.make_async_copy(low, low, fwd_recv.at[j]).wait()

        done = dot3(kw2, split(home[j].reshape(rows8, 256)))
        out_ref[:, 0, pl.ds(pl.multiple_of(j * 8, 8), 8), :] = done.reshape(8, 8, 256)
        return 0

    lax.fori_loop(0, 16, last, 0)

    @pl.when(v == 0)
    def _():
        def drain(j, _):
            forward(j).wait_send()
            return 0

        lax.fori_loop(0, 16, drain, 0)

    def drain_in(o, _):
        s_copy(o).wait_send()

        @pl.when(half == v)
        def _():
            pot_copy(o).wait_send()

        return 0

    lax.fori_loop(1, 16, drain_in, 0)

    @pl.when(half != v)
    def _():
        s_copy(0).wait_send()

    def drain_out(z, _):
        for w in range(2):
            @pl.when((v * 8 + z) * 2 + w != me)
            def _():
                out_copy(z, w).wait_send()

        return 0

    lax.fori_loop(0, 8, drain_out, 0)
    halo_drain(0, fs)
    halo_drain(1, f1)
    halo_drain(2, f2)


def fused(potential, start_basis):
    nb = start_basis.shape[0] * 2
    sites = 16 * start_basis.shape[1] * start_basis.shape[2] * start_basis.shape[3]
    sem = pltpu.SemaphoreType.DMA
    field = lambda planes: pltpu.VMEM((planes, nb, 8, 256), F32)
    return pl.pallas_call(
        functools.partial(kernel, nb, 1.0 / sites),
        out_shape=(
            jax.ShapeDtypeStruct(start_basis.shape, F32),
            jax.ShapeDtypeStruct((nb, nb), F32),
        ),
        in_specs=[pl.BlockSpec(memory_space=pl.ANY)] * 2,
        out_specs=(pl.BlockSpec(memory_space=pltpu.VMEM), pl.BlockSpec(memory_space=pltpu.VMEM)),
        scratch_shapes=[
            pltpu.VMEM((8, 8, 256), F32), pltpu.VMEM((8, 8, 256), F32),
            field(10), field(10), field(10), field(8), field(8),
            pltpu.VMEM((8, nb * 16, 256), BF16), pltpu.VMEM((8, nb * 16, 256), BF16),
            pltpu.VMEM((3, 2, 8, nb, 1, 256), F32), pltpu.VMEM((3, 2, 8, nb, 1, 256), F32),
            pltpu.VMEM((nb * 8, nb * 16), F32), pltpu.VMEM((nb * 16, nb * 16), F32),
            pltpu.VMEM((3, 8, nb, 128), F32), pltpu.VMEM((3, 4, nb, 128), F32), field(16),
            sem((16,)), sem((8, 2)), sem((16,)), sem((8,)),
            sem((3, 2, 8)), sem((3, 2, 8)), sem((3, 2)), sem((3, 2)),
            sem((3, 8)), sem((3, 8)), sem((3, 4)), sem((3, 4)), sem((8, 2)), sem((16,)),
            sem((16,)), sem((16,)),
        ],
        compiler_params=pltpu.CompilerParams(
            collective_id=0, has_side_effects=True, vmem_limit_bytes=48 * 2**20
        ),
        name="jacobi_davidson",
    )(potential, start_basis)


def solution(mesh):
    in_specs = (P("space", None, None), P("vec", "space", None, None))
    out_specs = (P("vec", "space", None, None), P())

    def body(potential, start_basis):
        fits = mesh.shape["space"] == 16 and mesh.shape["vec"] == 2
        if fits and start_basis.shape == (8, 1, 128, 256):
            return fused(potential, start_basis)
        return local(potential, start_basis)

    return jax.shard_map(body, mesh=mesh, in_specs=in_specs, out_specs=out_specs, check_vma=False)
```

```python
import functools

import jax
import jax.numpy as jnp
from jax import lax
from jax.experimental import pallas as pl
from jax.experimental.pallas import tpu as pltpu
from jax.sharding import PartitionSpec as P

NSWEEP = 3


SIGMA = 0.5
PREC = lax.Precision.HIGHEST


def extended(value, sides, width):
    for axis, dim in sides:
        peers, length = (lax.axis_size(axis), value.shape[dim])
        up = [(i, (i + 1) % peers) for i in range(peers)]
        down = [(j, i) for i, j in up]
        last = lax.slice_in_dim(value, length - width, length, axis=dim)
        first = lax.slice_in_dim(value, 0, width, axis=dim)
        before = lax.ppermute(last, axis, up)
        after = lax.ppermute(first, axis, down)
        value = jnp.concatenate([before, value, after], axis=dim)
    return value


def local_inner(left, right, scale):
    return jnp.einsum("kzyx,jzyx->kj", left, right, precision=PREC) * scale


def combine(coeff, vectors):
    return jnp.einsum("kj,kzyx->jzyx", coeff, vectors, precision=PREC)


def stencil(padded, potential):
    center = padded[:, 1:-1]
    beside = padded[:, 2:] + padded[:, :-2]
    beside = beside + jnp.roll(center, 1, 2) + jnp.roll(center, -1, 2)
    beside = beside + jnp.roll(center, 1, 3) + jnp.roll(center, -1, 3)
    return potential * center - beside


def inverse_factor(gram):
    lower = jnp.linalg.cholesky(gram)
    return jax.scipy.linalg.solve_triangular(
        lower, jnp.eye(gram.shape[0], dtype=jnp.float32), lower=True
    )


def local(potential, start_basis):
    mine = start_basis.shape[0]
    scale = 1.0 / (
        start_basis.shape[1] * start_basis.shape[2] * start_basis.shape[3] * lax.axis_size("space")
    )
    first = lax.axis_index("vec") * mine
    whole = lax.all_gather(start_basis, "vec", axis=0, tiled=True)
    gram = lax.psum(local_inner(whole, whole, scale), "space")
    basis_all = combine(inverse_factor(gram).T, whole)
    basis = lax.dynamic_slice_in_dim(basis_all, first, mine, 0)
    shifted = jnp.where(potential >= SIGMA, potential - SIGMA + 6.0, potential - SIGMA - 6.0)
    padded = extended(basis_all, (("space", 1),), 1)
    image_all = stencil(padded, potential)
    rayleigh = lax.psum(local_inner(basis_all, image_all, scale), "space")
    image = lax.dynamic_slice_in_dim(image_all, first, mine, 0)
    panel_mine = lax.dynamic_slice_in_dim(rayleigh, first, mine, 1)
    resid = image - combine(panel_mine, basis_all)
    correction = jnp.zeros_like(basis)
    for sweep in range(NSWEEP):
        coeff, cross = lax.psum(
            (local_inner(basis_all, correction, scale), local_inner(image_all, correction, scale)),
            "space",
        )
        padded = extended(correction, (("space", 1),), 1)
        proj = correction - combine(coeff, basis_all)
        moved = stencil(padded, potential) - combine(coeff, image_all) - SIGMA * proj
        back = cross - jnp.dot(rayleigh.T, coeff, precision=PREC)
        update = -resid - (moved - combine(back, basis_all))
        correction = correction + update / shifted
    proj_two = lax.psum(local_inner(basis_all, correction, scale), "space")
    fresh = correction - combine(proj_two, basis_all)
    fresh_all = lax.all_gather(fresh, "vec", axis=0, tiled=True)
    gram_two = lax.psum(local_inner(fresh_all, fresh_all, scale), "space")
    inverse_two = inverse_factor(gram_two)
    rows_mine = lax.dynamic_slice_in_dim(inverse_two, first, mine, 0)
    new_basis = combine(rows_mine.T, fresh_all)
    return (new_basis, rayleigh)


MESH = pl.DeviceIdType.MESH
F32 = jnp.float32
BF16 = jnp.bfloat16
NN = (((1,), (0,)), ((), ()))
NT = (((1,), (1,)), ((), ()))
TN = (((0,), (0,)), ((), ()))


def small(a, b, dims=NN):
    return lax.dot_general(a, b, dims, precision=PREC, preferred_element_type=F32)


def split(a):
    high = a.astype(BF16)
    return high, (a - high.astype(F32)).astype(BF16)


def dot3(a, b, dims=NN):
    (ah, al), (bh, bl) = a, b

    def one(p, q):
        return lax.dot_general(p, q, dims, preferred_element_type=F32)

    return one(ah, bh) + (one(ah, bl) + one(al, bh))


def tile_of(space):
    z, y, x = space // 4, (space // 2) % 2, space % 2
    q = 2 * y + (x + y) % 2
    return 4 * q + z + (q % 2) * (3 - 2 * z)


def space_of(tile):
    q, r = tile // 4, tile % 4
    z = r + (q % 2) * (3 - 2 * r)
    return z * 4 + (q // 2) * 2 + ((q + 1) // 2) % 2


def factor_inverse(gram):
    n = gram.shape[0]
    rows = lax.broadcasted_iota(jnp.int32, (n, n), 0)
    cols = lax.broadcasted_iota(jnp.int32, (n, n), 1)
    eye = jnp.where(rows == cols, 1.0, 0.0).astype(F32)
    upper, inv = gram, eye
    row = lax.broadcasted_iota(jnp.int32, (n, 1), 0)
    for k in range(n - 1):
        mult = jnp.where(row > k, upper[:, k : k + 1] / upper[k : k + 1, k : k + 1], 0.0)
        inv = inv - mult * inv[k : k + 1, :]
        upper = upper - mult * upper[k : k + 1, :]
    diag = jnp.sum(upper * eye, axis=1, keepdims=True)
    return inv / jnp.sqrt(diag)


def iota(shape, dim):
    return lax.broadcasted_iota(jnp.int32, shape, dim)


def one_pass(a, b, dims=NN):
    return lax.dot_general(a, b, dims, preferred_element_type=F32)


def exact(a):
    high, rest = a.astype(BF16), None
    rest = a - high.astype(F32)
    mid = rest.astype(BF16)
    return high, mid, (rest - mid.astype(F32)).astype(BF16)


def kron(matrix, transposed=False):
    a, b = matrix.shape[::-1] if transposed else matrix.shape
    rows = jnp.where(iota((8 * a, a), 0) // 8 == iota((8 * a, a), 1), 1.0, 0.0).astype(BF16)
    cols = jnp.where(iota((b, 8 * b), 0) == iota((b, 8 * b), 1) // 8, 1.0, 0.0).astype(BF16)
    same = iota((8 * a, 8 * b), 0) % 8 == iota((8 * a, 8 * b), 1) % 8

    def one(part):
        tall = one_pass(rows, part, NT if transposed else NN).astype(BF16)
        return jnp.where(same, one_pass(tall, cols), 0.0).astype(BF16)

    return tuple(one(part) for part in split(matrix))


def kernel(
    nb, scale,
    pot_in, s_in, out_ref, ray_ref,
    pot, dinv, fs, f1, f2, ft, fq, bih, bil, ysend, yrecv, acc_s, acc, red1, red2, home,
    in_send, in_recv, pot_send, pot_recv, y_sends, y_recvs, z_sends, z_recvs,
    r1_send, r1_recv, r2_send, r2_recv, out_send, out_recv, fwd_send, fwd_recv,
):
    s, v = lax.axis_index("space"), lax.axis_index("vec")
    tile = tile_of(s)
    half = s // 8
    me = s * 2 + v
    rows8 = nb * 8
    wide8 = 2 * rows8

    barrier = pltpu.get_barrier_semaphore()

    def greet(i, _):
        peer = (me + i) % 32
        pl.semaphore_signal(barrier, inc=1, device_id=(peer // 2, peer % 2), device_id_type=MESH)
        return 0

    lax.fori_loop(1, 32, greet, 0)
    pl.semaphore_wait(barrier, 31)

    def s_piece(dest):
        return s_in.at[:, 0, pl.ds(pl.multiple_of(tile_of(dest) * 8, 8), 8), :]

    s_slot = fs.at[1 + s % 8, pl.ds(v * 8, 8)]

    def pot_piece(dest):
        return pot_in.at[0, pl.ds(pl.multiple_of(tile_of(dest) * 8, 8), 8), :]

    def s_copy(o):
        dest = (s + o) % 16
        return pltpu.make_async_remote_copy(
            src_ref=s_piece(dest), dst_ref=s_slot,
            send_sem=in_send.at[o], recv_sem=in_recv.at[s % 8, v],
            device_id=(dest, half), device_id_type=MESH,
        )

    def pot_copy(o):
        dest = (s + o) % 16
        return pltpu.make_async_remote_copy(
            src_ref=pot_piece(dest), dst_ref=pot.at[s % 8],
            send_sem=pot_send.at[o], recv_sem=pot_recv.at[s % 8],
            device_id=(dest, half), device_id_type=MESH,
        )

    def send_in(o, _):
        s_copy(o).start()

        @pl.when(half == v)
        def _():
            pot_copy(o).start()

        return 0

    lax.fori_loop(1, 16, send_in, 0)

    @pl.when(half == v)
    def _():
        pltpu.make_async_copy(s_piece(s), s_slot, in_recv.at[s % 8, v]).start()
        pltpu.make_async_copy(pot_piece(s), pot.at[s % 8], pot_recv.at[s % 8]).start()

    @pl.when(half != v)
    def _():
        s_copy(0).start()


    after = space_of((tile + 1) % 16)
    before = space_of((tile + 15) % 16)

    def y_copies(n, z):
        return [
            pltpu.make_async_remote_copy(
                src_ref=ysend.at[n, i, z], dst_ref=yrecv.at[n, i, z],
                send_sem=y_sends.at[n, i, z], recv_sem=y_recvs.at[n, i, z],
                device_id=(device, v), device_id_type=MESH,
            )
            for i, device in enumerate((after, before))
        ]

    def z_copy(n, field, i):
        return pltpu.make_async_remote_copy(
            src_ref=field.at[(8, 1)[i]], dst_ref=field.at[(0, 9)[i]],
            send_sem=z_sends.at[n, i], recv_sem=z_recvs.at[n, i],
            device_id=(s, 1 - v), device_id_type=MESH,
        )

    def halo_start(n, field, z):
        ysend[n, 0, z] = field[1 + z, :, 7:8, :]
        ysend[n, 1, z] = field[1 + z, :, 0:1, :]
        for c in y_copies(n, z):
            c.start()

        @pl.when(z == 7)
        def _():
            z_copy(n, field, 0).start()

        @pl.when(z == 0)
        def _():
            z_copy(n, field, 1).start()

    def halo_wait(n, field, z):
        for c in y_copies(n, z):
            c.wait_recv()

        @pl.when(z == 0)
        def _():
            z_copy(n, field, 0).wait_recv()

        @pl.when(z == 7)
        def _():
            z_copy(n, field, 1).wait_recv()

    def halo_drain(n, field):
        def one(z, _):
            for c in y_copies(n, z):
                c.wait_send()
            return 0

        lax.fori_loop(0, 8, one, 0)
        z_copy(n, field, 0).wait_send()
        z_copy(n, field, 1).wait_send()

    def planes(body):
        def step(i, _):
            body((i + 7) % 8)
            return 0

        lax.fori_loop(0, 8, step, 0, unroll=2)

    inrow = iota((rows8, 256), 0) % 8
    is_first, is_last = inrow == 0, inrow == 7

    def flat(a):
        return jnp.broadcast_to(a, (nb, 8, 256)).reshape(rows8, 256)

    def get(field, z):
        return field[z].reshape(rows8, 256)

    def put(field, z, value):
        field[z] = value.reshape(nb, 8, 256)

    def apply_h(n, field, z):
        mid = get(field, z + 1)
        total = get(field, z) + get(field, z + 2)
        total += jnp.where(is_first, flat(yrecv[n, 0, z]), pltpu.roll(mid, 1, 0))
        total += jnp.where(is_last, flat(yrecv[n, 1, z]), pltpu.roll(mid, rows8 - 1, 0))
        total += pltpu.roll(mid, 1, 1) + pltpu.roll(mid, 255, 1)
        return mid, flat(pot[z][None]) * mid - total

    def squeeze(blocks):
        width = rows8 * len(blocks)
        wide = jnp.concatenate(blocks, axis=1)
        wide = jnp.where(iota((rows8, width), 0) % 8 == iota((rows8, width), 1) % 8, wide, 0.0)
        left = jnp.where(iota((nb, rows8), 0) == iota((nb, rows8), 1) // 8, 1.0, 0.0).astype(BF16)
        right = jnp.where(iota((width, 128), 0) // 8 == iota((width, 128), 1), 1.0, 0.0).astype(BF16)
        tall = sum(one_pass(left, part) for part in exact(wide))
        return sum(one_pass(part, right) for part in exact(tall)) * scale

    def total_of(n, blocks):
        rank = (s % 4) * 2 + v
        red1[n, rank] = squeeze(blocks)

        def copy1(i):
            peer = (rank + i) % 8
            return pltpu.make_async_remote_copy(
                src_ref=red1.at[n, rank], dst_ref=red1.at[n, rank],
                send_sem=r1_send.at[n, i], recv_sem=r1_recv.at[n, rank],
                device_id=((s // 4) * 4 + peer // 2, peer % 2), device_id_type=MESH,
            )

        def copy2(i):
            peer = (s // 4 + i) % 4
            return pltpu.make_async_remote_copy(
                src_ref=red2.at[n, s // 4], dst_ref=red2.at[n, s // 4],
                send_sem=r2_send.at[n, i], recv_sem=r2_recv.at[n, s // 4],
                device_id=(peer * 4 + s % 4, v), device_id_type=MESH,
            )

        def stage(copy, buf, recv, mine, count):
            for i in range(1, count):
                copy(i).start()
            for i in range(1, count):
                peer = (mine + i) % count
                slot = buf.at[n, peer]
                pltpu.make_async_copy(slot, slot, recv.at[n, peer]).wait()
            for i in range(1, count):
                copy(i).wait_send()
            total = buf[n, 0]
            for p in range(1, count):
                total = total + buf[n, p]
            return total

        red2[n, s // 4] = stage(copy1, red1, r1_recv, rank, 8)
        total = stage(copy2, red2, r2_recv, s // 4, 4)
        return [total[:, nb * i : nb * (i + 1)] for i in range(len(blocks))]

    acc_s[...] = jnp.zeros_like(acc_s)
    acc[...] = jnp.zeros_like(acc)

    def arrive(z):
        for w in range(2):
            slot = fs.at[1 + z, pl.ds(w * 8, 8)]
            pltpu.make_async_copy(slot, slot, in_recv.at[z, w]).wait()
        pltpu.make_async_copy(pot.at[z], pot.at[z], pot_recv.at[z]).wait()
        halo_start(0, fs, z)
        p = pot[z]
        inverse = 1.0 / jnp.where(p >= SIGMA, p - SIGMA + 6.0, p - SIGMA - 6.0)
        dinv[z] = inverse
        mid = get(fs, z + 1)
        both = jnp.concatenate([mid, flat(inverse[None]) * mid], axis=0)
        acc_s[...] += dot3(split(mid), split(both), NT)

    planes(arrive)

    def first(z):
        halo_wait(0, fs, z)
        mid, image = apply_h(0, fs, z)
        put(ft, z, image)
        left = jnp.concatenate([mid, image], axis=0)
        right = jnp.concatenate([image, flat(dinv[z][None]) * image], axis=0)
        acc[...] += dot3(split(left), split(right), NT)

    planes(first)
    lo, hi = slice(0, rows8), slice(rows8, wide8)
    gram, m0, raw, m1, m2 = total_of(
        0, [acc_s[:, lo], acc_s[:, hi], acc[lo, lo], acc[lo, hi], acc[hi, hi]]
    )
    w = factor_inverse(gram)

    def conj(m):
        return small(small(w, m), w, NT)

    def side(*parts):
        return jnp.concatenate(parts, axis=1)

    def stack(*parts):
        return jnp.concatenate(parts, axis=0)

    ray = conj(raw)
    zero = jnp.zeros_like(w)
    kbig = kron(stack(side(w, zero), side(zero, w), side(small(ray, w, TN), -w)))

    def second(z):
        mixed = dot3(kbig, split(stack(get(fs, z + 1), get(ft, z))))
        basis, image, resid = mixed[lo], mixed[hi], mixed[wide8:]
        put(f1, z + 1, flat(dinv[z][None]) * resid)
        halo_start(1, f1, z)
        high, low = split(stack(image, basis))
        bih[z] = high
        bil[z] = low

    planes(second)
    ray_ref[...] = ray
    n0, n1, n2 = conj(m0), conj(m1), conj(m2)
    coeff = small(n0, ray) - n1
    cross = small(n1, ray, TN) - n2
    edge = cross - small(ray, coeff, TN) - SIGMA * coeff
    kmix = kron(stack(coeff, edge), True)

    def third(z):
        halo_wait(1, f1, z)
        mid, image = apply_h(1, f1, z)
        mix = dot3(kmix, (bih[z], bil[z]))
        put(f2, z + 1, 2.0 * mid + flat(dinv[z][None]) * (SIGMA * mid - image + mix))
        halo_start(2, f2, z)

    planes(third)
    acc[...] = jnp.zeros_like(acc)

    def fourth(z):
        halo_wait(2, f2, z)
        mid, image = apply_h(2, f2, z)
        new = mid + get(f1, z + 1) + flat(dinv[z][None]) * (SIGMA * mid - image)
        put(fq, z, new)
        acc[...] += dot3((bih[z], bil[z]), split(stack(mid, new)), NT)

    planes(fourth)
    cross, coeff, part = total_of(1, [acc[lo, lo], acc[hi, lo], acc[hi, hi]])
    edge = cross - small(ray, coeff, TN) - SIGMA * coeff
    proj = part + small(n1, coeff) + small(n0, edge)
    klast = kron(stack(side(coeff, zero), side(edge, proj)), True)
    acc_s[...] = jnp.zeros_like(acc_s)

    @pl.when(v == 0)
    def _():
        for i in range(16):
            home[i, 8:16] = jnp.zeros((8, 8, 256), F32)

    def out_copy(z, w):
        return pltpu.make_async_remote_copy(
            src_ref=fq.at[z, pl.ds(w * 8, 8)], dst_ref=home.at[tile, pl.ds(w * 8, 8)],
            send_sem=out_send.at[z, w], recv_sem=out_recv.at[tile],
            device_id=(v * 8 + z, w), device_id_type=MESH,
        )

    def send_out(z):
        for w in range(2):
            mine = (v * 8 + z) * 2 + w == me

            @pl.when(mine)
            def _():
                pltpu.make_async_copy(
                    fq.at[z, pl.ds(w * 8, 8)], home.at[tile, pl.ds(w * 8, 8)], out_recv.at[tile]
                ).start()

            @pl.when(jnp.logical_not(mine))
            def _():
                out_copy(z, w).start()

    def fifth(i, _):
        z = (tile + i) % 8
        mixed = dot3(klast, (bih[z], bil[z]))
        fresh = get(fq, z) + flat(dinv[z][None]) * mixed[lo] - mixed[hi]
        put(fq, z, fresh)
        send_out(z)
        a = split(fresh)
        acc_s[:, lo] += dot3(a, a, NT)
        return 0

    lax.fori_loop(0, 8, fifth, 0, unroll=2)
    (gram2,) = total_of(2, [acc_s[:, lo]])
    w2 = factor_inverse(gram2)
    kw2 = kron(jnp.where(v == 0, w2[0:8], w2[8:16]))
    def forward(j):
        return pltpu.make_async_remote_copy(
            src_ref=home.at[j, pl.ds(0, 8)], dst_ref=home.at[j, pl.ds(0, 8)],
            send_sem=fwd_send.at[j], recv_sem=fwd_recv.at[j],
            device_id=(s, 1), device_id_type=MESH,
        )

    def last(i, _):
        j = (s + 32 - i // 2 - 8 * (i % 2)) % 16
        slot = home.at[j, pl.ds(v * 8, 8)]
        pltpu.make_async_copy(slot, slot, out_recv.at[j]).wait()

        @pl.when(v == 0)
        def _():
            forward(j).start()

        @pl.when(v == 1)
        def _():
            low = home.at[j, pl.ds(0, 8)]
            pltpu.make_async_copy(low, low, fwd_recv.at[j]).wait()

        done = dot3(kw2, split(home[j].reshape(rows8, 256)))
        out_ref[:, 0, pl.ds(pl.multiple_of(j * 8, 8), 8), :] = done.reshape(8, 8, 256)
        return 0

    lax.fori_loop(0, 16, last, 0, unroll=2)

    @pl.when(v == 0)
    def _():
        def drain(j, _):
            forward(j).wait_send()
            return 0

        lax.fori_loop(0, 16, drain, 0)

    def drain_in(o, _):
        s_copy(o).wait_send()

        @pl.when(half == v)
        def _():
            pot_copy(o).wait_send()

        return 0

    lax.fori_loop(1, 16, drain_in, 0)

    @pl.when(half != v)
    def _():
        s_copy(0).wait_send()

    def drain_out(z, _):
        for w in range(2):
            @pl.when((v * 8 + z) * 2 + w != me)
            def _():
                out_copy(z, w).wait_send()

        return 0

    lax.fori_loop(0, 8, drain_out, 0)
    halo_drain(0, fs)
    halo_drain(1, f1)
    halo_drain(2, f2)


def fused(potential, start_basis):
    nb = start_basis.shape[0] * 2
    sites = 16 * start_basis.shape[1] * start_basis.shape[2] * start_basis.shape[3]
    sem = pltpu.SemaphoreType.DMA
    field = lambda planes: pltpu.VMEM((planes, nb, 8, 256), F32)
    return pl.pallas_call(
        functools.partial(kernel, nb, 1.0 / sites),
        out_shape=(
            jax.ShapeDtypeStruct(start_basis.shape, F32),
            jax.ShapeDtypeStruct((nb, nb), F32),
        ),
        in_specs=[pl.BlockSpec(memory_space=pl.ANY)] * 2,
        out_specs=(pl.BlockSpec(memory_space=pltpu.VMEM), pl.BlockSpec(memory_space=pltpu.VMEM)),
        scratch_shapes=[
            pltpu.VMEM((8, 8, 256), F32), pltpu.VMEM((8, 8, 256), F32),
            field(10), field(10), field(10), field(8), field(8),
            pltpu.VMEM((8, nb * 16, 256), BF16), pltpu.VMEM((8, nb * 16, 256), BF16),
            pltpu.VMEM((3, 2, 8, nb, 1, 256), F32), pltpu.VMEM((3, 2, 8, nb, 1, 256), F32),
            pltpu.VMEM((nb * 8, nb * 16), F32), pltpu.VMEM((nb * 16, nb * 16), F32),
            pltpu.VMEM((3, 8, nb, 128), F32), pltpu.VMEM((3, 4, nb, 128), F32), field(16),
            sem((16,)), sem((8, 2)), sem((16,)), sem((8,)),
            sem((3, 2, 8)), sem((3, 2, 8)), sem((3, 2)), sem((3, 2)),
            sem((3, 8)), sem((3, 8)), sem((3, 4)), sem((3, 4)), sem((8, 2)), sem((16,)),
            sem((16,)), sem((16,)),
        ],
        compiler_params=pltpu.CompilerParams(
            collective_id=0, has_side_effects=True, vmem_limit_bytes=48 * 2**20
        ),
        name="jacobi_davidson",
    )(potential, start_basis)


def solution(mesh):
    in_specs = (P("space", None, None), P("vec", "space", None, None))
    out_specs = (P("vec", "space", None, None), P())

    def body(potential, start_basis):
        fits = mesh.shape["space"] == 16 and mesh.shape["vec"] == 2
        if fits and start_basis.shape == (8, 1, 128, 256):
            return fused(potential, start_basis)
        return local(potential, start_basis)

    return jax.shard_map(body, mesh=mesh, in_specs=in_specs, out_specs=out_specs, check_vma=False)
```
